512 devices in a mesh: dom: 32 (over y, x, core), own: 16 (over z).
Axes of the slice: x: 4, y: 4, z: 16, core: 2. Of those that a mesh axis runs over, the one named last changes fastest.
Arguments:
- tiles: bfloat16 [57344, 128, 128], P(('dom', 'own')), may hold values from -0.75 to 0.75
- prolong: bfloat16 [192, 128, 128], P('dom'), may hold values from -0.5 to 0.5
- features: bfloat16 [192, 128, 128], P('dom'), may hold values from -0.1875 to 0.1875
- match: int32 [192], P('dom'), may hold values from 0 to 2, as said below
- row_local: int32 [57344], P(('dom', 'own')), may hold values from 0 to 5
- col_dom: int32 [57344, 1], P(('dom', 'own')), may hold values from 0 to 31; in each aligned block of 112 rows (0 to 111, 112 to 223, ...) at most 4 rows name the same one
- col_local: int32 [57344], P(('dom', 'own')), may hold values from 0 to 5
- coarse_slot: int32 [57344], P(('dom', 'own')), may hold values from 0 to 31
- tile_count: int32 [512], P(('dom', 'own')), may hold values from 14 to 112, as said below
Outputs:
- coarse_tiles: float32 [1024, 128, 128], P(('dom', 'own'))
- coarse_features: float32 [12288, 128], P(('dom', 'own'))
The draws below stay inside these ranges and needn't reach their ends.
Inputs may be any that keep to these rules, and one draw needn't show every extreme that they name: `match`: within the 6 entries of each dom index every value appears exactly twice: the heavy-edge matching pairs fine blocks into coarse blocks. `col_dom`: among the 112 slots of one device at most 4 name the same dom index. `tile_count`: some device has all 112 slots live.
All inputs are finite; a program needn't handle non-finite values.
Results may differ from the reference program's by a relative error of at most 0.0029.
Values may be sent and summed in bfloat16 or wider, within the bound.
No kernel may reach another device: no remote copies, remote signals or barrier semaphores. Data moves between devices by JAX's collectives and lax.ppermute only.
A program may use at most 64 MiB of HBM per device.

```python
import math
import jax
import jax.numpy as jnp
import numpy as np
from jax import lax

TB = 128
F = 128
BD = 6
TD = 112
CAP = 4
NB = 192
TILES = 57344
CS = 32
N_DOM = 32
N_OWN = 16


def draw_match(key, part):
    key = jax.random.fold_in(key, 11)
    keys = jax.random.split(key, N_DOM)
    base = jnp.arange(BD, dtype=jnp.int32) // 2
    rows = jax.vmap(lambda k: jax.random.permutation(k, base))(keys)
    return rows.reshape(N_DOM * BD).astype(jnp.int32)


def draw_tile_count(key, part):
    key = jax.random.fold_in(key, 23)
    key_base, key_full, key_one = jax.random.split(key, 3)
    devices_all = N_DOM * N_OWN
    counts = jax.random.randint(key_base, (devices_all,), TD // 8, TD // 2 + 1, dtype=jnp.int32)
    full = jax.random.randint(key_full, (devices_all,), 0, 8, dtype=jnp.int32) == 0
    counts = jnp.where(full, TD, counts)
    chosen = jax.random.randint(key_one, (), 0, devices_all, dtype=jnp.int32)
    counts = jnp.where(jnp.arange(devices_all, dtype=jnp.int32) == chosen, TD, counts)
    return counts.astype(jnp.int32)


def place_ends(array, key, least, high):
    dims = array.shape
    spot = [jax.random.randint(jax.random.fold_in(key, axis), (), 0, dims[axis]) for axis in range(len(dims))]
    array = array.at[tuple(spot)].set(least)
    longest = dims.index(max(dims))
    spot[longest] = (spot[longest] + 1) % dims[longest]
    return array.at[tuple(spot)].set(high)


def block_levels(own_key, extent, cuts, low, top_value):
    loudness = 1.0
    for dim, shards_of in cuts:
        steps = jax.random.uniform(jax.random.fold_in(jax.random.fold_in(own_key, 6), dim), (shards_of,), jnp.float32, low / len(cuts), top_value / len(cuts))
        loudness = loudness * jnp.repeat(jnp.exp(steps), extent[dim] // shards_of).reshape((-1,) + (1,) * (len(extent) - 1 - dim))
    return loudness


def assign_block(rng, own, number, rows, amount, top, reach, lean):
    sequence = jax.random.permutation(rng, amount)
    crowded, ordinary = portions_of(amount, rows * top, reach, lean, True), portions_of(amount, rows * top, reach, lean, False)
    places = jnp.arange(amount)

    def named(sizes, turn):
        used = int((sizes > 0).sum())
        fixed = max(1, used // 4)
        passed = fixed + (places - fixed + turn * (used - fixed)) % max(1, amount - fixed)
        return jnp.zeros((amount,), jnp.int32).at[sequence[jnp.where(places < fixed, places, passed)]].set(jnp.asarray(sizes, jnp.int32))

    sizes = jnp.where(number % 4 == 0, named(crowded, number // 4), named(ordinary, number - number // 4 - 1))
    mixed = jax.random.permutation(jax.random.fold_in(own, 3), amount)
    giver, sink = mixed[0:amount // 2 * 2:2], mixed[1:amount // 2 * 2:2]
    room = jnp.minimum(sizes[giver] - 1, reach - sizes[sink]) // 2
    room = jnp.where((giver == sequence[0]) | (sink == sequence[0]) | (sizes[sink] == 0), 0, jnp.maximum(room, 0))
    passed = jax.random.randint(jax.random.fold_in(own, 4), (amount // 2,), 0, 1 << 20) % (room + 1)
    sizes = sizes.at[giver].add(-passed).at[sink].add(passed)
    labels = jnp.searchsorted(jnp.cumsum(sizes), jnp.arange(rows * top), side="right").astype(jnp.int32)
    grid = labels.reshape(top, rows).T
    grid = grid[jax.random.permutation(jax.random.fold_in(own, 1), rows)]
    turn = jax.random.randint(jax.random.fold_in(own, 2), (rows, 1), 0, top)
    return jnp.take_along_axis(grid, (jnp.arange(top)[None, :] + turn) % top, axis=1)


def portions_of(amount, total, most, lean, full):
    weights = [(1 << 20) // math.isqrt(grade ** lean) + 1 for grade in range(1, amount + 1)]
    largest = most if full else min(most, max(-(-total // amount), total * weights[0] // sum(weights)))
    least = 1 if total - largest >= amount - 1 else 0
    holding, surplus = [largest] + [least] * (amount - 1), total - largest - least * (amount - 1)
    while surplus > 0:
        free = [i for i in range(1, amount) if holding[i] < largest] or [i for i in range(1, amount) if holding[i] < most]
        mass, left = sum([weights[i] for i in free]), surplus
        for i in free:
            addition = min(most - holding[i], max(1, left * weights[i] // mass), surplus)
            holding[i] = holding[i] + addition
            surplus = surplus - addition
    return np.array(holding)


def bell_draw(key, extent, width, limit, shards=(), kind=jnp.bfloat16):
    gain = block_levels(key, extent, shards, -0.22, 0.18) if shards else 1.0
    values = jax.random.normal(key, extent, jnp.float32) * width * gain
    return jnp.minimum(jnp.maximum(values, -limit), limit).astype(kind)


def setup_inputs(seed: int = 0) -> dict:
    key_of = jax.random.split(jax.random.key(seed), 10)
    tiles = bell_draw(key_of[0], (TILES, TB, TB), 0.125, 0.75, ((0, 512),))
    prolong = bell_draw(key_of[1], (NB, TB, TB), TB ** -0.5, 0.5, ((0, 32),))
    features = bell_draw(key_of[2], (NB, TB, F), 0.03125, 0.1875, ((0, 32),))
    match = draw_match(jax.random.fold_in(key_of[9], 71), 0)
    row_local = place_ends(jax.random.randint(key_of[4], (TILES,), 0, BD), jax.random.fold_in(key_of[4], 1), 0, BD - 1).astype(jnp.int32)
    col_dom_keys = jax.random.split(jax.random.fold_in(key_of[5], 1), TILES // TD)
    col_dom_turns = jax.random.permutation(jax.random.fold_in(key_of[5], 3), TILES // TD)
    col_dom = jax.vmap(lambda own, number: assign_block(jax.random.fold_in(key_of[5], 2), own, number, TD, N_DOM, 1, CAP, 2))(col_dom_keys, col_dom_turns).reshape((TILES, 1))
    col_local = place_ends(jax.random.randint(key_of[6], (TILES,), 0, BD), jax.random.fold_in(key_of[6], 1), 0, BD - 1).astype(jnp.int32)
    coarse_slot = place_ends(jax.random.randint(key_of[7], (TILES,), 0, CS), jax.random.fold_in(key_of[7], 1), 0, CS - 1).astype(jnp.int32)
    tile_count = draw_tile_count(jax.random.fold_in(key_of[9], 71), 0)
    return {"tiles": tiles, "prolong": prolong, "features": features, "match": match, "row_local": row_local, "col_dom": col_dom, "col_local": col_local, "coarse_slot": coarse_slot, "tile_count": tile_count}


def reference(tiles, prolong, features, match, row_local, col_dom, col_local, coarse_slot, tile_count):
    groups = jnp.arange(N_DOM * N_OWN, dtype=jnp.int32)
    start_tiles = jnp.zeros((N_DOM * CS, TB, TB), jnp.float32)
    start_feats = jnp.zeros((N_DOM * (BD // 2), TB, F), jnp.float32)

    def step(carry, group):
        tile_sums, feat_sums = carry
        domain = group // N_OWN
        first = (group * TD).astype(jnp.int32)
        block_tiles = lax.dynamic_slice_in_dim(tiles, first, TD, 0).astype(jnp.float32)
        rows = lax.dynamic_slice_in_dim(row_local, first, TD, 0)
        targets = lax.dynamic_slice_in_dim(col_dom, first, TD, 0)[:, 0]
        locals_col = lax.dynamic_slice_in_dim(col_local, first, TD, 0)
        slots = lax.dynamic_slice_in_dim(coarse_slot, first, TD, 0)
        valid = (jnp.arange(TD, dtype=jnp.int32) < tile_count[group]).astype(jnp.float32)
        row_blocks = domain * BD + rows
        col_blocks = targets * BD + locals_col
        p_rows = prolong[row_blocks].astype(jnp.float32)
        left = jnp.einsum("tki,tkj->tij", p_rows, block_tiles, precision=lax.Precision.HIGHEST).astype(jnp.bfloat16)
        left = lax.optimization_barrier(left).astype(jnp.float32)
        p_cols = prolong[col_blocks].astype(jnp.float32)
        x_cols = features[col_blocks].astype(jnp.float32)
        right = jnp.einsum("tik,tkj->tij", left, p_cols, precision=lax.Precision.HIGHEST) * valid[:, None, None]
        feat = jnp.einsum("tik,tkf->tif", left, x_cols, precision=lax.Precision.HIGHEST) * valid[:, None, None]
        tile_sums = tile_sums.at[domain * CS + slots].add(right)
        coarse = domain * (BD // 2) + match[row_blocks]
        feat_sums = feat_sums.at[coarse].add(feat)
        return (tile_sums, feat_sums), None

    (tile_sums, feat_sums), _ = lax.scan(step, (start_tiles, start_feats), groups)
    return tile_sums, feat_sums.reshape(N_DOM * (BD // 2) * TB, F)
```

```python
import jax
import jax.numpy as jnp
from jax import lax
from jax.experimental import pallas as pl
from jax.experimental.pallas import tpu as pltpu
from jax.sharding import PartitionSpec as P

OWN = 16
STEP = 16
UNROLL = 4
BF = jnp.bfloat16
F32 = jnp.float32


def left_kernel(rows, count, prolong, tiles, left, turned):
    step = pl.program_id(0)

    @pl.when(step == 0)
    def _():
        for r in range(prolong.shape[0]):
            turned[r] = prolong[r].T

    @pl.when(step * STEP < count[0])
    def _():
        for k in range(STEP):
            row = rows[step * STEP + k]
            left[k] = jnp.dot(turned[row], tiles[k], preferred_element_type=F32).astype(BF)


def left_products(rows, count, prolong, tiles):
    total, width, _ = tiles.shape

    def block(i, rows, count):
        return (jnp.minimum(i, (count[0] - 1) // STEP), 0, 0)

    return pl.pallas_call(
        left_kernel,
        grid_spec=pltpu.PrefetchScalarGridSpec(
            num_scalar_prefetch=2,
            grid=(total // STEP,),
            in_specs=[
                pl.BlockSpec(prolong.shape, lambda i, rows, count: (0, 0, 0)),
                pl.BlockSpec((STEP, width, width), block),
            ],
            out_specs=pl.BlockSpec((STEP, width, width), block),
            scratch_shapes=[pltpu.VMEM(prolong.shape, BF)],
        ),
        out_shape=jax.ShapeDtypeStruct(tiles.shape, BF),
        compiler_params=pltpu.CompilerParams(vmem_limit_bytes=32 << 20),
        cost_estimate=pl.CostEstimate(flops=2 * total * width**3, bytes_accessed=4 * total * width**2, transcendentals=0),
        name="left_products",
    )(rows, count, prolong, tiles)


def column_kernel(where, slot, group, count, left, blocks, out, held_l, held_b, sums, feats, sem_l, sem_b):
    live = count[0]
    turns = pl.cdiv(live, UNROLL)

    def copies(t):
        return (
            pltpu.make_async_copy(left.at[t], held_l.at[t], sem_l.at[t]),
            pltpu.make_async_copy(blocks.at[where[t]], held_b.at[t], sem_b.at[t]),
        )

    @pl.loop(0, turns * UNROLL)
    def _(t):
        for c in copies(t):
            c.start()

    sums[...] = jnp.zeros_like(sums)
    feats[...] = jnp.zeros_like(feats)
    spare_slot = sums.shape[0] - 1
    spare_group = feats.shape[0] // 128 - 1

    @pl.loop(0, turns)
    def _(i):
        for u in range(UNROLL):
            for c in copies(i * UNROLL + u):
                c.wait()
        for u in range(UNROLL):
            t = i * UNROLL + u
            both = jnp.dot(held_l[t], held_b[t], preferred_element_type=F32)
            s = jnp.where(t < live, slot[t], spare_slot)
            g = jnp.where(t < live, group[t], spare_group)
            rows = pl.ds(pl.multiple_of(g * 128, 128), 128)
            sums[s] += both[:, :128]
            feats[rows, :] += both[:, 128:]

    for o in range(OWN):
        out[280 * o : 280 * o + 128, :] = sums[2 * o]
        out[280 * o + 128 : 280 * o + 256, :] = sums[2 * o + 1]
        out[280 * o + 256 : 280 * o + 280, :] = feats[24 * o : 24 * o + 24, :]


def column_products(where, slot, group, count, left, blocks):
    total = left.shape[0]
    smem = pl.BlockSpec(memory_space=pltpu.SMEM)
    return pl.pallas_call(
        column_kernel,
        in_specs=[smem] * 4 + [pl.BlockSpec(memory_space=pl.ANY)] * 2,
        out_specs=pl.BlockSpec(memory_space=pltpu.VMEM),
        out_shape=jax.ShapeDtypeStruct((OWN * 280, 128), F32),
        scratch_shapes=[
            pltpu.VMEM((total, 128, 128), BF),
            pltpu.VMEM((total, 128, 256), BF),
            pltpu.VMEM((33, 128, 128), F32),
            pltpu.VMEM((4 * 128, 128), F32),
            pltpu.SemaphoreType.DMA((total,)),
            pltpu.SemaphoreType.DMA((total,)),
        ],
        compiler_params=pltpu.CompilerParams(vmem_limit_bytes=48 << 20),
        cost_estimate=pl.CostEstimate(flops=4 * total * 128**3, bytes_accessed=12 << 20, transcendentals=0),
        name="column_products",
    )(where, slot, group, count, left, blocks)


def local(tiles, prolong, features, match, row_local, col_dom, col_local, coarse_slot, tile_count):
    here = prolong.shape[0]
    blocks = lax.all_gather(jnp.concatenate([prolong, features], axis=2), "dom", axis=0, tiled=True)
    left = left_products(row_local, tile_count, prolong, tiles)
    where = col_dom[:, 0] * here + col_local
    group = match[row_local]
    sums = column_products(where, coarse_slot, group, tile_count, left, blocks)
    mine = lax.psum_scatter(sums, "own", scatter_dimension=0, tiled=True)
    return mine[:256].reshape(2, 128, 128), mine[256:]


def solution(mesh):
    placed = (
        P(("dom", "own"), None, None),
        P("dom", None, None),
        P("dom", None, None),
        P("dom"),
        P(("dom", "own")),
        P(("dom", "own"), None),
        P(("dom", "own")),
        P(("dom", "own")),
        P(("dom", "own")),
    )
    return jax.shard_map(
        local,
        mesh=mesh,
        in_specs=placed,
        out_specs=(P(("dom", "own"), None, None), P(("dom", "own"), None)),
        check_vma=False,
    )
```

```python
import jax
import jax.numpy as jnp
from jax import lax
from jax.experimental import pallas as pl
from jax.experimental.pallas import tpu as pltpu
from jax.sharding import PartitionSpec as P

OWN = 16
HALF = OWN // 2
PART = 144
STEP = 16
UNROLL = 4
BF = jnp.bfloat16
F32 = jnp.float32


def left_kernel(rows, count, prolong, tiles, left, turned):
    step = pl.program_id(0)

    @pl.when(step == 0)
    def _():
        for r in range(prolong.shape[0]):
            turned[r] = prolong[r].T

    @pl.when(step * STEP < count[0])
    def _():
        for k in range(STEP):
            row = rows[step * STEP + k]
            left[k] = jnp.dot(turned[row], tiles[k], preferred_element_type=F32).astype(BF)


def left_products(rows, count, prolong, tiles):
    total, width, _ = tiles.shape

    def block(i, rows, count):
        return (jnp.minimum(i, (count[0] - 1) // STEP), 0, 0)

    return pl.pallas_call(
        left_kernel,
        grid_spec=pltpu.PrefetchScalarGridSpec(
            num_scalar_prefetch=2,
            grid=(total // STEP,),
            in_specs=[
                pl.BlockSpec(prolong.shape, lambda i, rows, count: (0, 0, 0)),
                pl.BlockSpec((STEP, width, width), block),
            ],
            out_specs=pl.BlockSpec((STEP, width, width), block),
            scratch_shapes=[pltpu.VMEM(prolong.shape, BF)],
        ),
        out_shape=jax.ShapeDtypeStruct(tiles.shape, BF),
        compiler_params=pltpu.CompilerParams(vmem_limit_bytes=32 << 20),
        cost_estimate=pl.CostEstimate(flops=2 * total * width**3, bytes_accessed=4 * total * width**2, transcendentals=0),
        name="left_products",
    )(rows, count, prolong, tiles)


def column_kernel(where, slot, group, count, parity, left, blocks, up, down, keep_a, keep_b, held_l, held_b, sums, feats, sem_l, sem_b):
    live = count[0]
    turns = pl.cdiv(live, UNROLL)

    def copies(t):
        return (
            pltpu.make_async_copy(left.at[t], held_l.at[t], sem_l.at[t]),
            pltpu.make_async_copy(blocks.at[where[t]], held_b.at[t], sem_b.at[t]),
        )

    @pl.loop(0, turns * UNROLL)
    def _(t):
        for c in copies(t):
            c.start()

    sums[...] = jnp.zeros_like(sums)
    feats[...] = jnp.zeros_like(feats)
    spare_slot = sums.shape[0] - 1
    spare_group = feats.shape[0] // 128 - 1

    @pl.loop(0, turns)
    def _(i):
        for u in range(UNROLL):
            for c in copies(i * UNROLL + u):
                c.wait()
        for u in range(UNROLL):
            t = i * UNROLL + u
            both = jnp.dot(held_l[t], held_b[t], preferred_element_type=F32)
            s = jnp.where(t < live, slot[t], spare_slot)
            g = jnp.where(t < live, group[t], spare_group)
            rows = pl.ds(pl.multiple_of(g * 128, 128), 128)
            sums[s] += both[:, :128]
            feats[rows, :] += both[:, 128:]

    p = parity[0]

    def put(ref, k, owner, part):
        ref[k, 0:128] = sums[2 * owner + part].astype(ref.dtype)
        rows = pl.ds(pl.multiple_of(24 * owner + 16 * part, 8), 16)
        ref[k, 128:144] = feats[rows, :].astype(ref.dtype)

    for k in range(HALF):
        put(up, k, 2 * k + 1 - p, p)
        put(down, k, 2 * k + 1 - p, 1 - p)
        put(keep_a, k, 2 * k + p, p)
        put(keep_b, k, 2 * k + p, 1 - p)


def column_products(where, slot, group, count, parity, left, blocks):
    total = left.shape[0]
    smem = pl.BlockSpec(memory_space=pltpu.SMEM)
    shape = (HALF, PART, 128)
    return pl.pallas_call(
        column_kernel,
        in_specs=[smem] * 5 + [pl.BlockSpec(memory_space=pl.ANY)] * 2,
        out_specs=[pl.BlockSpec(memory_space=pltpu.VMEM)] * 4,
        out_shape=[jax.ShapeDtypeStruct(shape, t) for t in (BF, BF, F32, F32)],
        scratch_shapes=[
            pltpu.VMEM((total, 128, 128), BF),
            pltpu.VMEM((total, 128, 256), BF),
            pltpu.VMEM((33, 128, 128), F32),
            pltpu.VMEM((4 * 128, 128), F32),
            pltpu.SemaphoreType.DMA((total,)),
            pltpu.SemaphoreType.DMA((total,)),
        ],
        compiler_params=pltpu.CompilerParams(vmem_limit_bytes=48 << 20),
        cost_estimate=pl.CostEstimate(flops=4 * total * 128**3, bytes_accessed=12 << 20, transcendentals=0),
        name="column_products",
    )(where, slot, group, count, parity, left, blocks)


def pair_kernel(keep_a, above, keep_b, below, out):
    out[:, :PART] = (keep_a[...] + above[...].astype(F32)).astype(BF)
    out[:, PART:] = (keep_b[...] + below[...].astype(F32)).astype(BF)


def pair_sums(keep_a, above, keep_b, below):
    return pl.pallas_call(
        pair_kernel,
        out_shape=jax.ShapeDtypeStruct((HALF, 2 * PART, 128), BF),
        compiler_params=pltpu.CompilerParams(vmem_limit_bytes=16 << 20),
        name="pair_sums",
    )(keep_a, above, keep_b, below)


def last_kernel(parity, parts, tiles, feats):
    p = parity[0]
    total = parts[0].astype(F32)
    for k in range(1, HALF):
        total += parts[k].astype(F32)
    tiles[p] = total[0:128]
    tiles[1 - p] = total[PART : PART + 128]
    first, second = total[128:PART], total[PART + 128 :]
    feats[0:16] = jnp.where(p == 0, first, second)
    feats[16:24] = jnp.where(p == 0, second, first)[0:8]


def last_sums(parity, parts):
    return pl.pallas_call(
        last_kernel,
        in_specs=[pl.BlockSpec(memory_space=pltpu.SMEM), pl.BlockSpec(memory_space=pltpu.VMEM)],
        out_specs=[pl.BlockSpec(memory_space=pltpu.VMEM)] * 2,
        out_shape=[jax.ShapeDtypeStruct((2, 128, 128), F32), jax.ShapeDtypeStruct((24, 128), F32)],
        compiler_params=pltpu.CompilerParams(vmem_limit_bytes=16 << 20),
        name="last_sums",
    )(parity, parts)


def own_sums(parity, up, down, keep_a, keep_b):
    below = lax.ppermute(up, "own", [(z, (z + 1) % OWN) for z in range(OWN)])
    above = lax.ppermute(down, "own", [(z, (z - 1) % OWN) for z in range(OWN)])
    mid = pair_sums(keep_a, above, keep_b, below)
    groups = [[2 * k + b for k in range(HALF)] for b in range(2)]
    parts = lax.all_to_all(mid, "own", 0, 0, tiled=True, axis_index_groups=groups)
    return last_sums(parity, parts)


def local(tiles, prolong, features, match, row_local, col_dom, col_local, coarse_slot, tile_count):
    here = prolong.shape[0]
    blocks = lax.all_gather(jnp.concatenate([prolong, features], axis=2), "dom", axis=0, tiled=True)
    left = left_products(row_local, tile_count, prolong, tiles)
    where = col_dom[:, 0] * here + col_local
    group = match[row_local]
    parity = jnp.reshape(lax.axis_index("own") % 2, (1,)).astype(jnp.int32)
    up, down, keep_a, keep_b = column_products(where, coarse_slot, group, tile_count, parity, left, blocks)
    return own_sums(parity, up, down, keep_a, keep_b)


def solution(mesh):
    placed = (
        P(("dom", "own"), None, None),
        P("dom", None, None),
        P("dom", None, None),
        P("dom"),
        P(("dom", "own")),
        P(("dom", "own"), None),
        P(("dom", "own")),
        P(("dom", "own")),
        P(("dom", "own")),
    )
    return jax.shard_map(
        local,
        mesh=mesh,
        in_specs=placed,
        out_specs=(P(("dom", "own"), None, None), P(("dom", "own"), None)),
        check_vma=False,
    )
```

```python
import functools

import jax
import jax.numpy as jnp
from jax import lax
from jax.experimental import pallas as pl
from jax.experimental.pallas import tpu as pltpu
from jax.sharding import PartitionSpec as P

OWN = 16
HALF = OWN // 2
CHUNK = 288
STEP = 16
UNROLL = 4
BF = jnp.bfloat16
F32 = jnp.float32


def left_kernel(rows, count, prolong, tiles, left, turned):
    step = pl.program_id(0)

    @pl.when(step == 0)
    def _():
        for r in range(prolong.shape[0]):
            turned[r] = prolong[r].T

    @pl.when(step * STEP < count[0])
    def _():
        for k in range(STEP):
            row = rows[step * STEP + k]
            left[k] = jnp.dot(turned[row], tiles[k], preferred_element_type=F32).astype(BF)


def left_products(rows, count, prolong, tiles):
    total, width, _ = tiles.shape

    def block(i, rows, count):
        return (jnp.minimum(i, (count[0] - 1) // STEP), 0, 0)

    return pl.pallas_call(
        left_kernel,
        grid_spec=pltpu.PrefetchScalarGridSpec(
            num_scalar_prefetch=2,
            grid=(total // STEP,),
            in_specs=[
                pl.BlockSpec(prolong.shape, lambda i, rows, count: (0, 0, 0)),
                pl.BlockSpec((STEP, width, width), block),
            ],
            out_specs=pl.BlockSpec((STEP, width, width), block),
            scratch_shapes=[pltpu.VMEM(prolong.shape, BF)],
        ),
        out_shape=jax.ShapeDtypeStruct(tiles.shape, BF),
        compiler_params=pltpu.CompilerParams(vmem_limit_bytes=32 << 20),
        cost_estimate=pl.CostEstimate(flops=2 * total * width**3, bytes_accessed=4 * total * width**2, transcendentals=0),
        name="left_products",
    )(rows, count, prolong, tiles)


def column_kernel(first, sources, kind, where, slot, group, count, parity, left, *rest):
    blocks, rest = rest[:sources], rest[sources:]
    if first:
        old_sums, old_feats, send, keep, held_l, held_b, sums, feats, order, sem_l, sem_b = rest
    else:
        sums, feats, held_l, held_b, order, sem_l, sem_b = rest
    live = count[0]
    spare_slot = sums.shape[0] - 1
    spare_group = feats.shape[0] // 128 - 1

    def choose(t, n):
        mine = (kind[t] >= first) & (kind[t] < first + sources)

        @pl.when(mine)
        def _():
            order[n] = t

        return n + mine.astype(jnp.int32)

    chosen = lax.fori_loop(0, live, choose, 0)
    turns = pl.cdiv(chosen, UNROLL)

    @pl.loop(chosen, turns * UNROLL)
    def _(n):
        order[n] = order[n - 1]

    @pl.loop(0, turns * UNROLL)
    def _(n):
        t = order[n]
        pltpu.make_async_copy(left.at[t], held_l.at[n], sem_l.at[n]).start()
        for k in range(sources):

            @pl.when(kind[t] == first + k)
            def _():
                pltpu.make_async_copy(blocks[k].at[where[t]], held_b.at[n], sem_b.at[n]).start()

    sums[...] = jnp.zeros_like(sums)
    feats[...] = jnp.zeros_like(feats)

    @pl.loop(0, turns)
    def _(i):
        for u in range(UNROLL):
            n = i * UNROLL + u
            pltpu.make_async_copy(left.at[0], held_l.at[n], sem_l.at[n]).wait()
            pltpu.make_async_copy(blocks[0].at[0], held_b.at[n], sem_b.at[n]).wait()
        for u in range(UNROLL):
            n = i * UNROLL + u
            t = order[n]
            both = jnp.dot(held_l[n], held_b[n], preferred_element_type=F32)
            s = jnp.where(n < chosen, slot[t], spare_slot)
            g = jnp.where(n < chosen, group[t], spare_group)
            rows = pl.ds(pl.multiple_of(g * 128, 128), 128)
            sums[s] += both[:, :128]
            feats[rows, :] += both[:, 128:]

    if not first:
        return
    p = parity[0]

    def put(ref, k, owner):
        for part in range(2):
            ref[k, 128 * part : 128 * part + 128] = (sums[2 * owner + part] + old_sums[2 * owner + part]).astype(ref.dtype)
        rows = pl.ds(pl.multiple_of(24 * owner, 8), 32)
        ref[k, 256:CHUNK] = (feats[rows, :] + old_feats[rows, :]).astype(ref.dtype)

    for k in range(HALF):
        put(send, k, 2 * k + 1 - p)
        put(keep, k, 2 * k + p)


def column_products(first, table, left, blocks, old=()):
    total = left.shape[0]
    smem = pl.BlockSpec(memory_space=pltpu.SMEM)
    vmem = pl.BlockSpec(memory_space=pltpu.VMEM)
    shape = (HALF, CHUNK, 128)
    held = [pltpu.VMEM((total, 128, 128), BF), pltpu.VMEM((total, 128, 256), BF)]
    sums = ((33, 128, 128), (4 * 128, 128))
    marks = [pltpu.SMEM((total + UNROLL,), jnp.int32), pltpu.SemaphoreType.DMA((total,)), pltpu.SemaphoreType.DMA((total,))]
    if first:
        outs = [jax.ShapeDtypeStruct(shape, t) for t in (BF, F32)]
        scratch = held + [pltpu.VMEM(s, F32) for s in sums] + marks
    else:
        outs = [jax.ShapeDtypeStruct(s, F32) for s in sums]
        scratch = held + marks
    return pl.pallas_call(
        functools.partial(column_kernel, first, len(blocks)),
        in_specs=[smem] * len(table) + [pl.BlockSpec(memory_space=pl.ANY)] * (1 + len(blocks)) + [vmem] * len(old),
        out_specs=[vmem] * len(outs),
        out_shape=outs,
        scratch_shapes=scratch,
        compiler_params=pltpu.CompilerParams(vmem_limit_bytes=48 << 20),
        cost_estimate=pl.CostEstimate(flops=2 * total * 128**3, bytes_accessed=6 << 20, transcendentals=0),
        name="column_products",
    )(*table, left, *blocks, *old)


def pair_kernel(keep, came, out):
    out[...] = (keep[...] + came[...].astype(F32)).astype(BF)


def pair_sums(keep, came):
    return pl.pallas_call(
        pair_kernel,
        out_shape=jax.ShapeDtypeStruct(keep.shape, BF),
        compiler_params=pltpu.CompilerParams(vmem_limit_bytes=16 << 20),
        name="pair_sums",
    )(keep, came)


def last_kernel(parts, tiles, feats):
    total = parts[0].astype(F32)
    for k in range(1, HALF):
        total += parts[k].astype(F32)
    tiles[0] = total[0:128]
    tiles[1] = total[128:256]
    feats[...] = total[256:280]


def last_sums(parts):
    return pl.pallas_call(
        last_kernel,
        out_shape=[jax.ShapeDtypeStruct((2, 128, 128), F32), jax.ShapeDtypeStruct((24, 128), F32)],
        compiler_params=pltpu.CompilerParams(vmem_limit_bytes=16 << 20),
        name="last_sums",
    )(parts)


def own_sums(send, keep):
    trade = []
    for d in range(32):
        for z in range(OWN):
            up = z % 2 == d % 2
            trade.append((d * OWN + z, d * OWN + (z + (1 if up else -1)) % OWN))
    mid = pair_sums(keep, lax.ppermute(send, ("dom", "own"), trade))
    groups = [[2 * k + b for k in range(HALF)] for b in range(2)]
    return last_sums(lax.all_to_all(mid, "own", 0, 0, tiled=True, axis_index_groups=groups))


def gather(pairs):
    over_x = [[[8 * y + 2 * x + c for x in range(4)] for y in range(4)] for c in range(2)]
    over_y = [[[8 * y + 2 * x + c for y in range(4)] for x in range(4)] for c in range(2)]
    for groups in (over_x[0] + over_y[1], over_y[0] + over_x[1]):
        pairs = lax.all_to_all(jnp.tile(pairs, (4, 1, 1)), "dom", 0, 0, tiled=True, axis_index_groups=groups)
    return pairs, lax.ppermute(pairs, "dom", [(i, i ^ 1) for i in range(32)])


def places(col_dom, col_local):
    y, x, core = col_dom // 8, col_dom // 2 % 4, col_dom % 2
    kind = jnp.where(core == lax.axis_index("dom") % 2, 0, 1)
    return kind, jnp.where(core == 0, y * 4 + x, x * 4 + y) * 6 + col_local


def local(tiles, prolong, features, match, row_local, col_dom, col_local, coarse_slot, tile_count):
    here, there = gather(jnp.concatenate([prolong, features], axis=2))
    left = left_products(row_local, tile_count, prolong, tiles)
    kind, where = places(col_dom[:, 0], col_local)
    parity = jnp.reshape(lax.axis_index("own") % 2, (1,)).astype(jnp.int32)
    table = (kind, where, coarse_slot, match[row_local], tile_count, parity)
    old = column_products(0, table, left, (here,))
    send, keep = column_products(1, table, left, (there,), old)
    return own_sums(send, keep)


def solution(mesh):
    placed = (
        P(("dom", "own"), None, None),
        P("dom", None, None),
        P("dom", None, None),
        P("dom"),
        P(("dom", "own")),
        P(("dom", "own"), None),
        P(("dom", "own")),
        P(("dom", "own")),
        P(("dom", "own")),
    )
    return jax.shard_map(
        local,
        mesh=mesh,
        in_specs=placed,
        out_specs=(P(("dom", "own"), None, None), P(("dom", "own"), None)),
        check_vma=False,
    )
```

```python
import jax
import jax.numpy as jnp
from jax import lax
from jax.experimental import pallas as pl
from jax.experimental.pallas import tpu as pltpu
from jax.sharding import PartitionSpec as P

OWN = 16
BD = 6
TD = 112
PLAN = 256
SPARE = 64
HALF = OWN // 2
CHUNK = 288
STEP = 16
UNROLL = 8
BF = jnp.bfloat16
F32 = jnp.float32


def copies_kernel(prolong, features, copies, held, sems):
    moves = [pltpu.make_async_copy(ref, held.at[k], sems.at[k]) for k, ref in enumerate((prolong, features))]
    for move in moves:
        move.start()
    for move in moves:
        move.wait()
    for k in range(4):
        for r in range(BD):
            copies[k * BD + r, :, 0:128] = held[0, r]
            copies[k * BD + r, :, 128:256] = held[1, r]


def four_copies(prolong, features):
    return pl.pallas_call(
        copies_kernel,
        in_specs=[pl.BlockSpec(memory_space=pltpu.HBM)] * 2,
        out_specs=pl.BlockSpec(memory_space=pltpu.VMEM),
        out_shape=jax.ShapeDtypeStruct((4 * BD, 128, 256), BF),
        scratch_shapes=[pltpu.VMEM((2,) + prolong.shape, BF), pltpu.SemaphoreType.DMA((2,))],
        compiler_params=pltpu.CompilerParams(vmem_limit_bytes=16 << 20),
        name="four_copies",
    )(prolong, features)


def left_kernel(rows, count, prolong, tiles, after, left, turned):
    step = pl.program_id(0)

    @pl.when(step == 0)
    def _():
        for r in range(BD):
            turned[r] = prolong[r].T

    @pl.when(step * STEP < count[0])
    def _():
        for k in range(STEP):
            row = rows[step * STEP + k]
            left[k] = jnp.dot(turned[row], tiles[k], preferred_element_type=F32).astype(BF)


def left_products(rows, count, prolong, tiles, after):
    total, width, _ = tiles.shape

    def block(i, rows, count):
        return (jnp.minimum(i, (count[0] - 1) // STEP), 0, 0)

    return pl.pallas_call(
        left_kernel,
        grid_spec=pltpu.PrefetchScalarGridSpec(
            num_scalar_prefetch=2,
            grid=(total // STEP,),
            in_specs=[pl.BlockSpec(prolong.shape, lambda i, rows, count: (0, 0, 0)), pl.BlockSpec((STEP, width, width), block), pl.BlockSpec(memory_space=pl.ANY)],
            out_specs=pl.BlockSpec((STEP, width, width), block),
            scratch_shapes=[pltpu.VMEM(prolong.shape, BF)],
        ),
        out_shape=jax.ShapeDtypeStruct(tiles.shape, BF),
        compiler_params=pltpu.CompilerParams(vmem_limit_bytes=48 << 20),
        cost_estimate=pl.CostEstimate(flops=2 * total * width**3, bytes_accessed=4 * total * width**2, transcendentals=0),
        name="left_products",
    )(rows, count, prolong, tiles, after)


def plan_kernel(place, mine, theirs, plan):
    start = place[0] * 96
    chosen = jnp.int32(0)
    for d, table in enumerate((mine, theirs)):

        def choose(t, n):
            at = table[0, t] - start
            plan[0, n] = d * TD + t
            plan[1, n] = jnp.clip(at, 0, 95)
            plan[2, n] = d * 32 + table[1, t]
            plan[3, n] = (d * 3 + table[3, table[2, t]]) * 128
            return n + ((at >= 0) & (at < 96)).astype(jnp.int32)

        chosen = lax.fori_loop(0, table[3, BD], choose, chosen)

    @pl.loop(chosen, chosen + UNROLL)
    def _(n):
        plan[0, n] = 0
        plan[1, n] = 0
        plan[2, n] = SPARE
        plan[3, n] = 6 * 128

    plan[0, PLAN - 1] = chosen
    plan[1, PLAN - 1] = mine[3, BD]
    plan[2, PLAN - 1] = theirs[3, BD]


def plan_products(place, mine, theirs):
    smem = pl.BlockSpec(memory_space=pltpu.SMEM)
    return pl.pallas_call(
        plan_kernel,
        in_specs=[smem] * 3,
        out_specs=smem,
        out_shape=jax.ShapeDtypeStruct((4, PLAN), jnp.int32),
        name="plan_products",
    )(place, mine, theirs)


def column_kernel(plan, left, left_theirs, blocks, keep, give, held_l, held_b, sums, feats, sems):
    moves = []
    for d, ref in enumerate((left, left_theirs)):
        for i in range(TD // STEP):
            move = pltpu.make_async_copy(ref.at[pl.ds(i * STEP, STEP)], held_l.at[pl.ds(d * TD + i * STEP, STEP)], sems.at[len(moves)])
            moves.append((i * STEP < plan[1 + d, PLAN - 1], move))
    moves.append((True, pltpu.make_async_copy(blocks, held_b, sems.at[len(moves)])))
    for live, move in moves:
        pl.when(live)(move.start)
    sums[...] = jnp.zeros_like(sums)
    feats[...] = jnp.zeros_like(feats)
    for live, move in moves:
        pl.when(live)(move.wait)

    @pl.loop(0, pl.cdiv(plan[0, PLAN - 1], UNROLL))
    def _(i):
        for u in range(UNROLL):
            n = i * UNROLL + u
            both = jnp.dot(held_l[plan[0, n]], held_b[plan[1, n]], preferred_element_type=F32)
            rows = pl.ds(pl.multiple_of(plan[3, n], 128), 128)
            sums[plan[2, n]] += both[:, :128]
            feats[rows, :] += both[:, 128:]

    for d, ref in enumerate((keep, give)):
        for o in range(OWN):
            for part in range(2):
                ref[o, 128 * part : 128 * part + 128] = sums[32 * d + 2 * o + part].astype(ref.dtype)
            ref[o, 256:CHUNK] = feats[384 * d + 24 * o : 384 * d + 24 * o + 32, :].astype(ref.dtype)


def column_products(plan, left, left_theirs, blocks):
    vmem = pl.BlockSpec(memory_space=pltpu.VMEM)
    return pl.pallas_call(
        column_kernel,
        in_specs=[pl.BlockSpec(memory_space=pltpu.SMEM)] + [pl.BlockSpec(memory_space=pltpu.HBM)] * 3,
        out_specs=[vmem] * 2,
        out_shape=[jax.ShapeDtypeStruct((OWN, CHUNK, 128), t) for t in (F32, BF)],
        scratch_shapes=[
            pltpu.VMEM((2 * TD, 128, 128), BF),
            pltpu.VMEM(blocks.shape, BF),
            pltpu.VMEM((SPARE + 1, 128, 128), F32),
            pltpu.VMEM((7 * 128, 128), F32),
            pltpu.SemaphoreType.DMA((2 * TD // STEP + 1,)),
        ],
        compiler_params=pltpu.CompilerParams(vmem_limit_bytes=40 << 20),
        cost_estimate=pl.CostEstimate(flops=4 * TD * 128**3, bytes_accessed=18 << 20, transcendentals=0),
        name="column_products",
    )(plan, left, left_theirs, blocks)


def fold_kernel(place, keep, came, stay, send):
    p = place[1]
    for k in range(HALF):
        here, there = 2 * k + p, 2 * k + 1 - p
        stay[k] = keep[here] + came[here].astype(F32)
        send[k] = (keep[there] + came[there].astype(F32)).astype(BF)


def fold_sums(place, keep, came):
    vmem = pl.BlockSpec(memory_space=pltpu.VMEM)
    return pl.pallas_call(
        fold_kernel,
        in_specs=[pl.BlockSpec(memory_space=pltpu.SMEM), vmem, vmem],
        out_specs=[vmem] * 2,
        out_shape=[jax.ShapeDtypeStruct((HALF, CHUNK, 128), t) for t in (F32, BF)],
        compiler_params=pltpu.CompilerParams(vmem_limit_bytes=24 << 20),
        name="fold_sums",
    )(place, keep, came)


def pair_kernel(keep, came, out):
    out[...] = (keep[...] + came[...].astype(F32)).astype(BF)


def pair_sums(keep, came):
    return pl.pallas_call(
        pair_kernel,
        out_shape=jax.ShapeDtypeStruct(keep.shape, BF),
        compiler_params=pltpu.CompilerParams(vmem_limit_bytes=16 << 20),
        name="pair_sums",
    )(keep, came)


def last_kernel(parts, tiles, feats):
    total = parts[0].astype(F32)
    for k in range(1, HALF):
        total += parts[k].astype(F32)
    tiles[0] = total[0:128]
    tiles[1] = total[128:256]
    feats[...] = total[256:280]


def last_sums(parts):
    return pl.pallas_call(
        last_kernel,
        out_shape=[jax.ShapeDtypeStruct((2, 128, 128), F32), jax.ShapeDtypeStruct((24, 128), F32)],
        compiler_params=pltpu.CompilerParams(vmem_limit_bytes=16 << 20),
        name="last_sums",
    )(parts)


def own_sums(send, keep):
    trade = []
    for d in range(32):
        for z in range(OWN):
            up = z % 2 == d % 2
            trade.append((d * OWN + z, d * OWN + (z + (1 if up else -1)) % OWN))
    mid = pair_sums(keep, lax.ppermute(send, ("dom", "own"), trade))
    groups = [[2 * k + b for k in range(HALF)] for b in range(2)]
    return last_sums(lax.all_to_all(mid, "own", 0, 0, tiled=True, axis_index_groups=groups))


def gather(copies):
    over_x = [[[8 * y + 2 * x + c for x in range(4)] for y in range(4)] for c in range(2)]
    over_y = [[[8 * y + 2 * x + c for y in range(4)] for x in range(4)] for c in range(2)]
    nearby = lax.all_to_all(copies, "dom", 0, 0, tiled=True, axis_index_groups=over_x[0] + over_y[1])
    copies = jnp.tile(nearby, (4, 1, 1))
    return lax.all_to_all(copies, "dom", 0, 0, tiled=True, axis_index_groups=over_y[0] + over_x[1])


def places(col_dom, col_local):
    y, x, core = col_dom // 8, col_dom // 2 % 4, col_dom % 2
    return 96 * core + jnp.where(core == 0, y * 4 + x, x * 4 + y) * BD + col_local


def local(tiles, prolong, features, match, row_local, col_dom, col_local, coarse_slot, tile_count):
    copies = four_copies(prolong, features)
    left = left_products(row_local, tile_count, prolong, tiles, copies)
    last = jnp.concatenate([match, tile_count, jnp.zeros((tiles.shape[0] - BD - 1,), jnp.int32)])
    mine = jnp.stack([places(col_dom[:, 0], col_local), coarse_slot, row_local, last])
    swap = [(i, i ^ 1) for i in range(32)]
    theirs, left_theirs = lax.ppermute(mine, "dom", swap), lax.ppermute(left, "dom", swap)
    blocks = gather(copies)
    place = jnp.stack([lax.axis_index("dom") % 2, lax.axis_index("own") % 2]).astype(jnp.int32)
    plan = plan_products(place, mine, theirs)
    keep, give = column_products(plan, left, left_theirs, blocks)
    stay, send = fold_sums(place, keep, lax.ppermute(give, "dom", swap))
    return own_sums(send, stay)


def solution(mesh):
    placed = (
        P(("dom", "own"), None, None),
        P("dom", None, None),
        P("dom", None, None),
        P("dom"),
        P(("dom", "own")),
        P(("dom", "own"), None),
        P(("dom", "own")),
        P(("dom", "own")),
        P(("dom", "own")),
    )
    return jax.shard_map(
        local,
        mesh=mesh,
        in_specs=placed,
        out_specs=(P(("dom", "own"), None, None), P(("dom", "own"), None)),
        check_vma=False,
    )
```

```python
import jax
import jax.numpy as jnp
from jax import lax
from jax.experimental import pallas as pl
from jax.experimental.pallas import tpu as pltpu
from jax.sharding import PartitionSpec as P

OWN = 16
BD = 6
TD = 112
PLAN = 256
SPARE = 64
HALF = OWN // 2
CHUNK = 288
STEP = 16
UNROLL = 16
BF = jnp.bfloat16
ORDER = [[[0, 1, 2, 3, 4, 5, 6, 7], [4, 5, 6, 7, 0, 1, 2, 3]], [[4, 5, 6, 7, 0, 1, 2, 3], [0, 1, 2, 3, 4, 5, 6, 7]]]
F32 = jnp.float32


def left_kernel(rows, count, prolong, tiles, after, left, turned):
    step = pl.program_id(0)

    @pl.when(step == 0)
    def _():
        for r in range(BD):
            turned[r] = prolong[r].T

    @pl.when(step * STEP < count[0])
    def _():
        for k in range(STEP):
            row = rows[step * STEP + k]
            left[k] = jnp.dot(turned[row], tiles[k], preferred_element_type=F32).astype(BF)


def left_products(rows, count, prolong, tiles, after):
    total, width, _ = tiles.shape

    def block(i, rows, count):
        return (jnp.minimum(i, (count[0] - 1) // STEP), 0, 0)

    return pl.pallas_call(
        left_kernel,
        grid_spec=pltpu.PrefetchScalarGridSpec(
            num_scalar_prefetch=2,
            grid=(total // STEP,),
            in_specs=[pl.BlockSpec(prolong.shape, lambda i, rows, count: (0, 0, 0)), pl.BlockSpec((STEP, width, width), block), pl.BlockSpec(memory_space=pl.ANY)],
            out_specs=pl.BlockSpec((STEP, width, width), block),
            scratch_shapes=[pltpu.VMEM(prolong.shape, BF)],
        ),
        out_shape=jax.ShapeDtypeStruct(tiles.shape, BF),
        compiler_params=pltpu.CompilerParams(vmem_limit_bytes=48 << 20),
        cost_estimate=pl.CostEstimate(flops=2 * total * width**3, bytes_accessed=4 * total * width**2, transcendentals=0),
        name="left_products",
    )(rows, count, prolong, tiles, after)


def again_kernel(nearby, out):
    out[0] = nearby[...]


def four_times(nearby):
    each = nearby.shape[0]
    out = pl.pallas_call(
        again_kernel,
        grid=(2, 4),
        in_specs=[pl.BlockSpec((each // 2,) + nearby.shape[1:], lambda i, k: (i, 0, 0))],
        out_specs=pl.BlockSpec((1, each // 2) + nearby.shape[1:], lambda i, k: (k, i, 0, 0)),
        out_shape=jax.ShapeDtypeStruct((4,) + nearby.shape, BF),
        compiler_params=pltpu.CompilerParams(vmem_limit_bytes=16 << 20),
        name="four_times",
    )(nearby)
    return out.reshape((4 * each,) + nearby.shape[1:])


def plan_kernel(place, mine, theirs, plan):
    start = place[0] * 96
    chosen = jnp.int32(0)
    for d, table in enumerate((mine, theirs)):

        def choose(t, n):
            at = table[0, t] - start
            plan[0, n] = d * TD + t
            plan[1, n] = jnp.clip(at, 0, 95)
            plan[2, n] = d * 32 + table[1, t]
            plan[3, n] = (d * 3 + table[3, table[2, t]]) * 128
            return n + ((at >= 0) & (at < 96)).astype(jnp.int32)

        chosen = lax.fori_loop(0, table[3, BD], choose, chosen)

    @pl.loop(chosen, chosen + UNROLL)
    def _(n):
        plan[0, n] = 0
        plan[1, n] = 0
        plan[2, n] = SPARE
        plan[3, n] = 6 * 128

    plan[0, PLAN - 1] = chosen
    plan[1, PLAN - 1] = mine[3, BD]
    plan[2, PLAN - 1] = theirs[3, BD]


def plan_products(place, mine, theirs):
    smem = pl.BlockSpec(memory_space=pltpu.SMEM)
    return pl.pallas_call(
        plan_kernel,
        in_specs=[smem] * 3,
        out_specs=smem,
        out_shape=jax.ShapeDtypeStruct((4, PLAN), jnp.int32),
        name="plan_products",
    )(place, mine, theirs)


def column_kernel(planned, left, left_theirs, blocks, keep, give, plan, held_l, held_b, sums, feats, sems):
    table = pltpu.make_async_copy(planned, plan, sems.at[0])
    table.start()
    whole = pltpu.make_async_copy(blocks, held_b, sems.at[1])
    whole.start()
    table.wait()
    moves = []
    for d, ref in enumerate((left, left_theirs)):
        for i in range(TD // STEP):
            move = pltpu.make_async_copy(ref.at[pl.ds(i * STEP, STEP)], held_l.at[pl.ds(d * TD + i * STEP, STEP)], sems.at[2 + len(moves)])
            moves.append((i * STEP < plan[1 + d, PLAN - 1], move))
    for live, move in moves:
        pl.when(live)(move.start)
    sums[...] = jnp.zeros_like(sums)
    feats[...] = jnp.zeros_like(feats)
    for live, move in moves:
        pl.when(live)(move.wait)
    whole.wait()

    @pl.loop(0, pl.cdiv(plan[0, PLAN - 1], UNROLL))
    def _(i):
        for u in range(UNROLL):
            n = i * UNROLL + u
            both = jnp.dot(held_l[plan[0, n]], held_b[plan[1, n]], preferred_element_type=F32)
            rows = pl.ds(pl.multiple_of(plan[3, n], 128), 128)
            sums[plan[2, n]] += both[:, :128]
            feats[rows, :] += both[:, 128:]

    for d, ref in enumerate((keep, give)):
        for o in range(OWN):
            for part in range(2):
                ref[o, 128 * part : 128 * part + 128] = sums[32 * d + 2 * o + part].astype(ref.dtype)
            ref[o, 256:CHUNK] = feats[384 * d + 24 * o : 384 * d + 24 * o + 32, :].astype(ref.dtype)


def column_products(plan, left, left_theirs, blocks):
    vmem = pl.BlockSpec(memory_space=pltpu.VMEM)
    return pl.pallas_call(
        column_kernel,
        in_specs=[pl.BlockSpec(memory_space=pltpu.HBM)] * 4,
        out_specs=[vmem] * 2,
        out_shape=[jax.ShapeDtypeStruct((OWN, CHUNK, 128), t) for t in (F32, BF)],
        scratch_shapes=[
            pltpu.SMEM(plan.shape, jnp.int32),
            pltpu.VMEM((2 * TD, 128, 128), BF),
            pltpu.VMEM(blocks.shape, BF),
            pltpu.VMEM((SPARE + 1, 128, 128), F32),
            pltpu.VMEM((7 * 128, 128), F32),
            pltpu.SemaphoreType.DMA((2 * TD // STEP + 2,)),
        ],
        compiler_params=pltpu.CompilerParams(vmem_limit_bytes=40 << 20),
        cost_estimate=pl.CostEstimate(flops=4 * TD * 128**3, bytes_accessed=18 << 20, transcendentals=0),
        name="column_products",
    )(plan, left, left_theirs, blocks)


def fold_kernel(place, keep, came, stay, send):
    p = place[1]
    for k in range(HALF):
        here, there = 2 * k + p, 2 * k + 1 - p
        stay[k] = keep[here] + came[here].astype(F32)
        send[k] = (keep[there] + came[there].astype(F32)).astype(BF)


def fold_sums(place, keep, came):
    vmem = pl.BlockSpec(memory_space=pltpu.VMEM)
    return pl.pallas_call(
        fold_kernel,
        in_specs=[pl.BlockSpec(memory_space=pltpu.SMEM), vmem, vmem],
        out_specs=[vmem] * 2,
        out_shape=[jax.ShapeDtypeStruct((HALF, CHUNK, 128), t) for t in (F32, BF)],
        compiler_params=pltpu.CompilerParams(vmem_limit_bytes=24 << 20),
        name="fold_sums",
    )(place, keep, came)


def pair_kernel(place, keep, came, out):
    for core in range(2):
        for parity in range(2):

            @pl.when((place[0] == core) & (place[1] == parity))
            def _():
                for k, j in enumerate(ORDER[core][parity]):
                    out[k] = (keep[j] + came[j].astype(F32)).astype(BF)


def pair_sums(place, keep, came):
    vmem = pl.BlockSpec(memory_space=pltpu.VMEM)
    return pl.pallas_call(
        pair_kernel,
        in_specs=[pl.BlockSpec(memory_space=pltpu.SMEM), vmem, vmem],
        out_shape=jax.ShapeDtypeStruct(keep.shape, BF),
        compiler_params=pltpu.CompilerParams(vmem_limit_bytes=16 << 20),
        name="pair_sums",
    )(place, keep, came)


def last_kernel(parts, tiles, feats):
    total = parts[0].astype(F32)
    for k in range(1, HALF):
        total += parts[k].astype(F32)
    tiles[0] = total[0:128]
    tiles[1] = total[128:256]
    feats[...] = total[256:280]


def last_sums(parts):
    return pl.pallas_call(
        last_kernel,
        out_shape=[jax.ShapeDtypeStruct((2, 128, 128), F32), jax.ShapeDtypeStruct((24, 128), F32)],
        compiler_params=pltpu.CompilerParams(vmem_limit_bytes=16 << 20),
        name="last_sums",
    )(parts)


def own_sums(place, send, keep):
    trade = []
    for d in range(32):
        for z in range(OWN):
            up = z % 2 == d % 2
            trade.append((d * OWN + z, d * OWN + (z + (1 if up else -1)) % OWN))
    mid = pair_sums(place, keep, lax.ppermute(send, ("dom", "own"), trade))
    groups = []
    for d in range(32):
        groups += [[d * OWN + 2 * k + b for k in ORDER[d % 2][b]] for b in range(2)]
    return last_sums(lax.all_to_all(mid, ("dom", "own"), 0, 0, tiled=True, axis_index_groups=groups))


def gather(copies):
    over_x = [[[8 * y + 2 * x + c for x in range(4)] for y in range(4)] for c in range(2)]
    over_y = [[[8 * y + 2 * x + c for y in range(4)] for x in range(4)] for c in range(2)]
    nearby = lax.all_to_all(copies, "dom", 0, 0, tiled=True, axis_index_groups=over_x[0] + over_y[1])
    copies = four_times(nearby)
    return lax.all_to_all(copies, "dom", 0, 0, tiled=True, axis_index_groups=over_y[0] + over_x[1])


def places(col_dom, col_local):
    y, x, core = col_dom // 8, col_dom // 2 % 4, col_dom % 2
    return 96 * core + jnp.where(core == 0, y * 4 + x, x * 4 + y) * BD + col_local


def local(tiles, prolong, features, match, row_local, col_dom, col_local, coarse_slot, tile_count):
    copies = jnp.tile(jnp.concatenate([prolong, features], axis=2), (4, 1, 1))
    left = left_products(row_local, tile_count, prolong, tiles, copies)
    last = jnp.concatenate([match, tile_count, jnp.zeros((tiles.shape[0] - BD - 1,), jnp.int32)])
    mine = jnp.stack([places(col_dom[:, 0], col_local), coarse_slot, row_local, last])
    swap = [(i, i ^ 1) for i in range(32)]
    theirs, left_theirs = lax.ppermute(mine, "dom", swap), lax.ppermute(left, "dom", swap)
    blocks = gather(copies)
    place = jnp.stack([lax.axis_index("dom") % 2, lax.axis_index("own") % 2]).astype(jnp.int32)
    plan = plan_products(place, mine, theirs)
    keep, give = column_products(plan, left, left_theirs, blocks)
    stay, send = fold_sums(place, keep, lax.ppermute(give, "dom", swap))
    return own_sums(place, send, stay)


def solution(mesh):
    placed = (
        P(("dom", "own"), None, None),
        P("dom", None, None),
        P("dom", None, None),
        P("dom"),
        P(("dom", "own")),
        P(("dom", "own"), None),
        P(("dom", "own")),
        P(("dom", "own")),
        P(("dom", "own")),
    )
    return jax.shard_map(
        local,
        mesh=mesh,
        in_specs=placed,
        out_specs=(P(("dom", "own"), None, None), P(("dom", "own"), None)),
        check_vma=False,
    )
```

```python
import jax
import jax.numpy as jnp
from jax import lax
from jax.experimental import pallas as pl
from jax.experimental.pallas import tpu as pltpu
from jax.sharding import PartitionSpec as P

OWN = 16
BD = 6
TD = 112
PLAN = 256
SPARE = 64
HALF = OWN // 2
CHUNK = 288
STEP = 16
UNROLL = 16
BF = jnp.bfloat16
ORDER = [[[0, 1, 2, 3, 4, 5, 6, 7], [4, 5, 6, 7, 0, 1, 2, 3]], [[4, 5, 6, 7, 0, 1, 2, 3], [0, 1, 2, 3, 4, 5, 6, 7]]]
F32 = jnp.float32


def left_kernel(rows, count, prolong, tiles, after, left, turned):
    step = pl.program_id(0)

    @pl.when(step == 0)
    def _():
        for r in range(BD):
            turned[r] = prolong[r].T

    @pl.when(step * STEP < count[0])
    def _():
        for k in range(STEP):
            row = rows[step * STEP + k]
            left[k] = jnp.dot(turned[row], tiles[k], preferred_element_type=F32).astype(BF)


def left_products(rows, count, prolong, tiles, after):
    total, width, _ = tiles.shape

    def block(i, rows, count):
        return (jnp.minimum(i, (count[0] - 1) // STEP), 0, 0)

    return pl.pallas_call(
        left_kernel,
        grid_spec=pltpu.PrefetchScalarGridSpec(
            num_scalar_prefetch=2,
            grid=(total // STEP,),
            in_specs=[pl.BlockSpec(prolong.shape, lambda i, rows, count: (0, 0, 0)), pl.BlockSpec((STEP, width, width), block), pl.BlockSpec(memory_space=pl.ANY)],
            out_specs=pl.BlockSpec((STEP, width, width), block),
            scratch_shapes=[pltpu.VMEM(prolong.shape, BF)],
        ),
        out_shape=jax.ShapeDtypeStruct(tiles.shape, BF),
        compiler_params=pltpu.CompilerParams(vmem_limit_bytes=48 << 20),
        cost_estimate=pl.CostEstimate(flops=2 * total * width**3, bytes_accessed=4 * total * width**2, transcendentals=0),
        name="left_products",
    )(rows, count, prolong, tiles, after)


def again_kernel(nearby, out):
    out[0] = nearby[...]


def four_times(nearby):
    each = nearby.shape[0]
    out = pl.pallas_call(
        again_kernel,
        grid=(2, 4),
        in_specs=[pl.BlockSpec((each // 2,) + nearby.shape[1:], lambda i, k: (i, 0, 0))],
        out_specs=pl.BlockSpec((1, each // 2) + nearby.shape[1:], lambda i, k: (k, i, 0, 0)),
        out_shape=jax.ShapeDtypeStruct((4,) + nearby.shape, BF),
        compiler_params=pltpu.CompilerParams(vmem_limit_bytes=16 << 20),
        name="four_times",
    )(nearby)
    return out.reshape((4 * each,) + nearby.shape[1:])


def plan_kernel(place, mine, theirs, plan):
    start = place[0] * 96
    chosen = jnp.int32(0)
    for d, table in enumerate((mine, theirs)):

        def choose(t, n):
            at = table[0, t] - start
            plan[0, n] = d * TD + t
            plan[1, n] = jnp.clip(at, 0, 95)
            plan[2, n] = d * 32 + table[1, t]
            plan[3, n] = (d * 3 + table[3, table[2, t]]) * 128
            return n + ((at >= 0) & (at < 96)).astype(jnp.int32)

        chosen = lax.fori_loop(0, table[3, BD], choose, chosen)

    @pl.loop(chosen, chosen + UNROLL)
    def _(n):
        plan[0, n] = 0
        plan[1, n] = 0
        plan[2, n] = SPARE
        plan[3, n] = 6 * 128

    plan[0, PLAN - 1] = chosen
    plan[1, PLAN - 1] = mine[3, BD]
    plan[2, PLAN - 1] = theirs[3, BD]


def plan_products(place, mine, theirs):
    smem = pl.BlockSpec(memory_space=pltpu.SMEM)
    return pl.pallas_call(
        plan_kernel,
        in_specs=[smem] * 3,
        out_specs=smem,
        out_shape=jax.ShapeDtypeStruct((4, PLAN), jnp.int32),
        name="plan_products",
    )(place, mine, theirs)


def column_kernel(planned, left, left_theirs, blocks, keep, give, plan, held_l, held_b, sums, feats, sems):
    table = pltpu.make_async_copy(planned, plan, sems.at[0])
    table.start()
    whole = pltpu.make_async_copy(blocks, held_b, sems.at[1])
    whole.start()
    table.wait()
    moves = []
    for d, ref in enumerate((left, left_theirs)):
        for i in range(TD // STEP):
            move = pltpu.make_async_copy(ref.at[pl.ds(i * STEP, STEP)], held_l.at[pl.ds(d * TD + i * STEP, STEP)], sems.at[2 + len(moves)])
            moves.append((i * STEP < plan[1 + d, PLAN - 1], move))
    for live, move in moves:
        pl.when(live)(move.start)
    sums[...] = jnp.zeros_like(sums)
    feats[...] = jnp.zeros_like(feats)
    for live, move in moves:
        pl.when(live)(move.wait)
    whole.wait()

    @pl.loop(0, pl.cdiv(plan[0, PLAN - 1], UNROLL))
    def _(i):
        for u in range(UNROLL):
            n = i * UNROLL + u
            both = jnp.dot(held_l[plan[0, n]], held_b[plan[1, n]], preferred_element_type=F32)
            rows = pl.ds(pl.multiple_of(plan[3, n], 128), 128)
            sums[plan[2, n]] += both[:, :128]
            feats[rows, :] += both[:, 128:]

    for d, ref in enumerate((keep, give)):
        for o in range(OWN):
            for part in range(2):
                ref[o, 128 * part : 128 * part + 128] = sums[32 * d + 2 * o + part].astype(ref.dtype)
            ref[o, 256:CHUNK] = feats[384 * d + 24 * o : 384 * d + 24 * o + 32, :].astype(ref.dtype)


def column_products(plan, left, left_theirs, blocks):
    vmem = pl.BlockSpec(memory_space=pltpu.VMEM)
    return pl.pallas_call(
        column_kernel,
        in_specs=[pl.BlockSpec(memory_space=pltpu.HBM)] * 4,
        out_specs=[vmem] * 2,
        out_shape=[jax.ShapeDtypeStruct((OWN, CHUNK, 128), t) for t in (F32, BF)],
        scratch_shapes=[
            pltpu.SMEM(plan.shape, jnp.int32),
            pltpu.VMEM((2 * TD, 128, 128), BF),
            pltpu.VMEM(blocks.shape, BF),
            pltpu.VMEM((SPARE + 1, 128, 128), F32),
            pltpu.VMEM((7 * 128, 128), F32),
            pltpu.SemaphoreType.DMA((2 * TD // STEP + 2,)),
        ],
        compiler_params=pltpu.CompilerParams(vmem_limit_bytes=40 << 20),
        cost_estimate=pl.CostEstimate(flops=4 * TD * 128**3, bytes_accessed=18 << 20, transcendentals=0),
        name="column_products",
    )(plan, left, left_theirs, blocks)


def fold_kernel(place, keep, came, stay, send):
    for core in range(2):
        for p in range(2):

            @pl.when((place[0] == core) & (place[1] == p))
            def _():
                for k in range(HALF):
                    here, there = 2 * ORDER[core][p][k] + p, 2 * ORDER[core][1 - p][k] + 1 - p
                    stay[k] = keep[here] + came[here].astype(F32)
                    send[k] = (keep[there] + came[there].astype(F32)).astype(BF)


def fold_sums(place, keep, came):
    vmem = pl.BlockSpec(memory_space=pltpu.VMEM)
    return pl.pallas_call(
        fold_kernel,
        in_specs=[pl.BlockSpec(memory_space=pltpu.SMEM), vmem, vmem],
        out_specs=[vmem] * 2,
        out_shape=[jax.ShapeDtypeStruct((HALF, CHUNK, 128), t) for t in (F32, BF)],
        compiler_params=pltpu.CompilerParams(vmem_limit_bytes=24 << 20),
        name="fold_sums",
    )(place, keep, came)


def pair_kernel(keep, came, out):
    out[...] = (keep[...] + came[...].astype(F32)).astype(BF)


def pair_sums(keep, came):
    return pl.pallas_call(
        pair_kernel,
        out_shape=jax.ShapeDtypeStruct(keep.shape, BF),
        compiler_params=pltpu.CompilerParams(vmem_limit_bytes=16 << 20),
        name="pair_sums",
    )(keep, came)


def last_kernel(parts, tiles, feats):
    total = parts[0].astype(F32)
    for k in range(1, HALF):
        total += parts[k].astype(F32)
    tiles[0] = total[0:128]
    tiles[1] = total[128:256]
    feats[...] = total[256:280]


def last_sums(parts):
    return pl.pallas_call(
        last_kernel,
        out_shape=[jax.ShapeDtypeStruct((2, 128, 128), F32), jax.ShapeDtypeStruct((24, 128), F32)],
        compiler_params=pltpu.CompilerParams(vmem_limit_bytes=16 << 20),
        name="last_sums",
    )(parts)


def own_sums(send, keep):
    trade = []
    for d in range(32):
        for z in range(OWN):
            up = z % 2 == d % 2
            trade.append((d * OWN + z, d * OWN + (z + (1 if up else -1)) % OWN))
    mid = pair_sums(keep, lax.ppermute(send, ("dom", "own"), trade))
    groups = []
    for d in range(32):
        groups += [[d * OWN + 2 * k + b for k in ORDER[d % 2][b]] for b in range(2)]
    return last_sums(lax.all_to_all(mid, ("dom", "own"), 0, 0, tiled=True, axis_index_groups=groups))


def gather(copies):
    over_x = [[[8 * y + 2 * x + c for x in range(4)] for y in range(4)] for c in range(2)]
    over_y = [[[8 * y + 2 * x + c for y in range(4)] for x in range(4)] for c in range(2)]
    nearby = lax.all_to_all(copies, "dom", 0, 0, tiled=True, axis_index_groups=over_x[0] + over_y[1])
    copies = four_times(nearby)
    return lax.all_to_all(copies, "dom", 0, 0, tiled=True, axis_index_groups=over_y[0] + over_x[1])


def places(col_dom, col_local):
    y, x, core = col_dom // 8, col_dom // 2 % 4, col_dom % 2
    return 96 * core + jnp.where(core == 0, y * 4 + x, x * 4 + y) * BD + col_local


def local(tiles, prolong, features, match, row_local, col_dom, col_local, coarse_slot, tile_count):
    copies = jnp.tile(jnp.concatenate([prolong, features], axis=2), (4, 1, 1))
    left = left_products(row_local, tile_count, prolong, tiles, copies)
    last = jnp.concatenate([match, tile_count, jnp.zeros((tiles.shape[0] - BD - 1,), jnp.int32)])
    mine = jnp.stack([places(col_dom[:, 0], col_local), coarse_slot, row_local, last])
    swap = [(i, i ^ 1) for i in range(32)]
    theirs, left_theirs = lax.ppermute(mine, "dom", swap), lax.ppermute(left, "dom", swap)
    blocks = gather(copies)
    place = jnp.stack([lax.axis_index("dom") % 2, lax.axis_index("own") % 2]).astype(jnp.int32)
    plan = plan_products(place, mine, theirs)
    keep, give = column_products(plan, left, left_theirs, blocks)
    stay, send = fold_sums(place, keep, lax.ppermute(give, "dom", swap))
    return own_sums(send, stay)


def solution(mesh):
    placed = (
        P(("dom", "own"), None, None),
        P("dom", None, None),
        P("dom", None, None),
        P("dom"),
        P(("dom", "own")),
        P(("dom", "own"), None),
        P(("dom", "own")),
        P(("dom", "own")),
        P(("dom", "own")),
    )
    return jax.shard_map(
        local,
        mesh=mesh,
        in_specs=placed,
        out_specs=(P(("dom", "own"), None, None), P(("dom", "own"), None)),
        check_vma=False,
    )
```

```python
import jax
import jax.numpy as jnp
from jax import lax
from jax.experimental import pallas as pl
from jax.experimental.pallas import tpu as pltpu
from jax.sharding import PartitionSpec as P

OWN = 16
BD = 6
TD = 112
PLAN = 256
SPARE = 64
HALF = OWN // 2
CHUNK = 288
STEP = 16
UNROLL = 16
REST = 4
BF = jnp.bfloat16
ORDER = [[[0, 1, 2, 3, 4, 5, 6, 7], [4, 5, 6, 7, 0, 1, 2, 3]], [[4, 5, 6, 7, 0, 1, 2, 3], [0, 1, 2, 3, 4, 5, 6, 7]]]
F32 = jnp.float32


def left_kernel(rows, count, prolong, tiles, after, left, turned):
    step = pl.program_id(0)

    @pl.when(step == 0)
    def _():
        for r in range(BD):
            turned[r] = prolong[r].T

    @pl.when(step * STEP < count[0])
    def _():
        for k in range(STEP):
            row = rows[step * STEP + k]
            left[k] = jnp.dot(turned[row], tiles[k], preferred_element_type=F32).astype(BF)


def left_products(rows, count, prolong, tiles, after):
    total, width, _ = tiles.shape

    def block(i, rows, count):
        return (jnp.minimum(i, (count[0] - 1) // STEP), 0, 0)

    return pl.pallas_call(
        left_kernel,
        grid_spec=pltpu.PrefetchScalarGridSpec(
            num_scalar_prefetch=2,
            grid=(total // STEP,),
            in_specs=[pl.BlockSpec(prolong.shape, lambda i, rows, count: (0, 0, 0)), pl.BlockSpec((STEP, width, width), block), pl.BlockSpec(memory_space=pl.ANY)],
            out_specs=pl.BlockSpec((STEP, width, width), block),
            scratch_shapes=[pltpu.VMEM(prolong.shape, BF)],
        ),
        out_shape=jax.ShapeDtypeStruct(tiles.shape, BF),
        compiler_params=pltpu.CompilerParams(vmem_limit_bytes=48 << 20),
        cost_estimate=pl.CostEstimate(flops=2 * total * width**3, bytes_accessed=4 * total * width**2, transcendentals=0),
        name="left_products",
    )(rows, count, prolong, tiles, after)


def again_kernel(nearby, out):
    out[0] = nearby[...]


def four_times(nearby):
    each = nearby.shape[0]
    out = pl.pallas_call(
        again_kernel,
        grid=(2, 4),
        in_specs=[pl.BlockSpec((each // 2,) + nearby.shape[1:], lambda i, k: (i, 0, 0))],
        out_specs=pl.BlockSpec((1, each // 2) + nearby.shape[1:], lambda i, k: (k, i, 0, 0)),
        out_shape=jax.ShapeDtypeStruct((4,) + nearby.shape, BF),
        compiler_params=pltpu.CompilerParams(vmem_limit_bytes=16 << 20),
        name="four_times",
    )(nearby)
    return out.reshape((4 * each,) + nearby.shape[1:])


def plan_kernel(place, mine, theirs, plan):
    start = place[0] * 96
    chosen = jnp.int32(0)
    for d, table in enumerate((mine, theirs)):

        def choose(t, n):
            at = table[0, t] - start
            plan[0, n] = d * TD + t
            plan[1, n] = jnp.clip(at, 0, 95)
            plan[2, n] = d * 32 + table[1, t]
            plan[3, n] = (d * 3 + table[3, table[2, t]]) * 128
            return n + ((at >= 0) & (at < 96)).astype(jnp.int32)

        chosen = lax.fori_loop(0, table[3, BD], choose, chosen)

    @pl.loop(chosen, chosen + UNROLL)
    def _(n):
        plan[0, n] = 0
        plan[1, n] = 0
        plan[2, n] = SPARE
        plan[3, n] = 6 * 128

    plan[0, PLAN - 1] = chosen
    plan[1, PLAN - 1] = mine[3, BD]
    plan[2, PLAN - 1] = theirs[3, BD]


def plan_products(place, mine, theirs):
    smem = pl.BlockSpec(memory_space=pltpu.SMEM)
    return pl.pallas_call(
        plan_kernel,
        in_specs=[smem] * 3,
        out_specs=smem,
        out_shape=jax.ShapeDtypeStruct((4, PLAN), jnp.int32),
        name="plan_products",
    )(place, mine, theirs)


def column_kernel(planned, left, left_theirs, blocks, keep, give, plan, held_l, held_b, sums, feats, sems):
    table = pltpu.make_async_copy(planned, plan, sems.at[0])
    table.start()
    whole = pltpu.make_async_copy(blocks, held_b, sems.at[1])
    whole.start()
    table.wait()
    moves = []
    for d, ref in enumerate((left, left_theirs)):
        for i in range(TD // STEP):
            move = pltpu.make_async_copy(ref.at[pl.ds(i * STEP, STEP)], held_l.at[pl.ds(d * TD + i * STEP, STEP)], sems.at[2 + len(moves)])
            moves.append((i * STEP < plan[1 + d, PLAN - 1], move))
    for live, move in moves:
        pl.when(live)(move.start)
    sums[...] = jnp.zeros_like(sums)
    feats[...] = jnp.zeros_like(feats)
    for live, move in moves:
        pl.when(live)(move.wait)
    whole.wait()

    def add(first, number):
        for u in range(number):
            n = first + u
            both = jnp.dot(held_l[plan[0, n]], held_b[plan[1, n]], preferred_element_type=F32)
            rows = pl.ds(pl.multiple_of(plan[3, n], 128), 128)
            sums[plan[2, n]] += both[:, :128]
            feats[rows, :] += both[:, 128:]

    chosen = plan[0, PLAN - 1]
    full = chosen // UNROLL

    @pl.loop(0, full)
    def _(i):
        add(i * UNROLL, UNROLL)

    @pl.loop(0, pl.cdiv(chosen - full * UNROLL, REST))
    def _(i):
        add(full * UNROLL + i * REST, REST)

    for d, ref in enumerate((keep, give)):
        for o in range(OWN):
            for part in range(2):
                ref[o, 128 * part : 128 * part + 128] = sums[32 * d + 2 * o + part].astype(ref.dtype)
            ref[o, 256:CHUNK] = feats[384 * d + 24 * o : 384 * d + 24 * o + 32, :].astype(ref.dtype)


def column_products(plan, left, left_theirs, blocks):
    vmem = pl.BlockSpec(memory_space=pltpu.VMEM)
    return pl.pallas_call(
        column_kernel,
        in_specs=[pl.BlockSpec(memory_space=pltpu.HBM)] * 4,
        out_specs=[vmem] * 2,
        out_shape=[jax.ShapeDtypeStruct((OWN, CHUNK, 128), t) for t in (F32, BF)],
        scratch_shapes=[
            pltpu.SMEM(plan.shape, jnp.int32),
            pltpu.VMEM((2 * TD, 128, 128), BF),
            pltpu.VMEM(blocks.shape, BF),
            pltpu.VMEM((SPARE + 1, 128, 128), F32),
            pltpu.VMEM((7 * 128, 128), F32),
            pltpu.SemaphoreType.DMA((2 * TD // STEP + 2,)),
        ],
        compiler_params=pltpu.CompilerParams(vmem_limit_bytes=40 << 20),
        cost_estimate=pl.CostEstimate(flops=4 * TD * 128**3, bytes_accessed=18 << 20, transcendentals=0),
        name="column_products",
    )(plan, left, left_theirs, blocks)


def fold_kernel(place, keep, came, stay, send):
    for core in range(2):
        for p in range(2):

            @pl.when((place[0] == core) & (place[1] == p))
            def _():
                for k in range(HALF):
                    here, there = 2 * ORDER[core][p][k] + p, 2 * ORDER[core][1 - p][k] + 1 - p
                    stay[k] = keep[here] + came[here].astype(F32)
                    send[k] = (keep[there] + came[there].astype(F32)).astype(BF)


def fold_sums(place, keep, came):
    vmem = pl.BlockSpec(memory_space=pltpu.VMEM)
    return pl.pallas_call(
        fold_kernel,
        in_specs=[pl.BlockSpec(memory_space=pltpu.SMEM), vmem, vmem],
        out_specs=[vmem] * 2,
        out_shape=[jax.ShapeDtypeStruct((HALF, CHUNK, 128), t) for t in (F32, BF)],
        compiler_params=pltpu.CompilerParams(vmem_limit_bytes=24 << 20),
        name="fold_sums",
    )(place, keep, came)


def pair_kernel(keep, came, out):
    out[...] = (keep[...] + came[...].astype(F32)).astype(BF)


def pair_sums(keep, came):
    return pl.pallas_call(
        pair_kernel,
        out_shape=jax.ShapeDtypeStruct(keep.shape, BF),
        compiler_params=pltpu.CompilerParams(vmem_limit_bytes=16 << 20),
        name="pair_sums",
    )(keep, came)


def last_kernel(parts, tiles, feats):
    total = parts[0].astype(F32)
    for k in range(1, HALF):
        total += parts[k].astype(F32)
    tiles[0] = total[0:128]
    tiles[1] = total[128:256]
    feats[...] = total[256:280]


def last_sums(parts):
    return pl.pallas_call(
        last_kernel,
        out_shape=[jax.ShapeDtypeStruct((2, 128, 128), F32), jax.ShapeDtypeStruct((24, 128), F32)],
        compiler_params=pltpu.CompilerParams(vmem_limit_bytes=16 << 20),
        name="last_sums",
    )(parts)


def own_sums(send, keep):
    trade = []
    for d in range(32):
        for z in range(OWN):
            up = z % 2 == d % 2
            trade.append((d * OWN + z, d * OWN + (z + (1 if up else -1)) % OWN))
    mid = pair_sums(keep, lax.ppermute(send, ("dom", "own"), trade))
    groups = []
    for d in range(32):
        groups += [[d * OWN + 2 * k + b for k in ORDER[d % 2][b]] for b in range(2)]
    return last_sums(lax.all_to_all(mid, ("dom", "own"), 0, 0, tiled=True, axis_index_groups=groups))


def gather(copies):
    over_x = [[[8 * y + 2 * x + c for x in range(4)] for y in range(4)] for c in range(2)]
    over_y = [[[8 * y + 2 * x + c for y in range(4)] for x in range(4)] for c in range(2)]
    nearby = lax.all_to_all(copies, "dom", 0, 0, tiled=True, axis_index_groups=over_x[0] + over_y[1])
    copies = four_times(nearby)
    return lax.all_to_all(copies, "dom", 0, 0, tiled=True, axis_index_groups=over_y[0] + over_x[1])


def places(col_dom, col_local):
    y, x, core = col_dom // 8, col_dom // 2 % 4, col_dom % 2
    return 96 * core + jnp.where(core == 0, y * 4 + x, x * 4 + y) * BD + col_local


def local(tiles, prolong, features, match, row_local, col_dom, col_local, coarse_slot, tile_count):
    copies = jnp.tile(jnp.concatenate([prolong, features], axis=2), (4, 1, 1))
    left = left_products(row_local, tile_count, prolong, tiles, copies)
    last = jnp.concatenate([match, tile_count, jnp.zeros((tiles.shape[0] - BD - 1,), jnp.int32)])
    mine = jnp.stack([places(col_dom[:, 0], col_local), coarse_slot, row_local, last])
    swap = [(i, i ^ 1) for i in range(32)]
    theirs, left_theirs = lax.ppermute(mine, "dom", swap), lax.ppermute(left, "dom", swap)
    blocks = gather(copies)
    place = jnp.stack([lax.axis_index("dom") % 2, lax.axis_index("own") % 2]).astype(jnp.int32)
    plan = plan_products(place, mine, theirs)
    keep, give = column_products(plan, left, left_theirs, blocks)
    stay, send = fold_sums(place, keep, lax.ppermute(give, "dom", swap))
    return own_sums(send, stay)


def solution(mesh):
    placed = (
        P(("dom", "own"), None, None),
        P("dom", None, None),
        P("dom", None, None),
        P("dom"),
        P(("dom", "own")),
        P(("dom", "own"), None),
        P(("dom", "own")),
        P(("dom", "own")),
        P(("dom", "own")),
    )
    return jax.shard_map(
        local,
        mesh=mesh,
        in_specs=placed,
        out_specs=(P(("dom", "own"), None, None), P(("dom", "own"), None)),
        check_vma=False,
    )
```
